256 devices in a mesh: seq: 64 (over x, z_hi, y, core), head: 4 (over z_lo).
Axes of the slice: x: 4, y: 4, z: 8 (z_hi: 2, z_lo: 4; z = z_hi * 4 + z_lo), core: 2. Of those that a mesh axis runs over, the one named last changes fastest.
Arguments:
- queries: bfloat16 [12288, 4096], P('seq', 'head'), may hold values from -150 to 150
- keys: bfloat16 [12288, 1024], P('seq', 'head'), may hold values from -6 to 6
- values: bfloat16 [12288, 1024], P('seq', 'head'), may hold values from -6 to 6
- out_weight: bfloat16 [4096, 4096], P('head'), may hold values from -0.5 to 0.5
Outputs:
- projected: bfloat16 [12288, 4096], P('seq', 'head')
The draws below stay inside these ranges and needn't reach their ends.
All inputs are finite; a program needn't handle non-finite values.
Results may differ from the reference program's by a relative error of at most 0.015.
Values may be sent and summed in bfloat16 or wider, within the bound.
No kernel may reach another device: no remote copies, remote signals or barrier semaphores. Data moves between devices by JAX's collectives and lax.ppermute only.
A program may use at most 128 MiB of HBM per device.

```python
import math
import jax
import jax.numpy as jnp
from jax import lax

D = 4096
HEADS = 32
KV_HEADS = 8
HEAD_DIM = 128
TOK_DEV = 192
SEQ = 12288


def shared_keys(key):
    drawn = jax.random.normal(key, (SEQ, KV_HEADS * HEAD_DIM), jnp.float32)
    return jnp.clip(drawn, -6.0, 6.0)


def draw_keys(key, part):
    key_base = shared_keys(key)
    return key_base.astype(jnp.bfloat16)


def draw_queries(key, part):
    key = jax.random.fold_in(key, 5)
    fresh_draw = jnp.clip(jax.random.normal(key, (SEQ, HEADS * HEAD_DIM), jnp.float32), -6.0, 6.0)
    return fresh_draw.astype(jnp.bfloat16)


def block_levels(rng, extent, cuts, smallest, high):
    gain = 1.0
    for position, shards_of in cuts:
        heights = jax.random.uniform(jax.random.fold_in(jax.random.fold_in(rng, 6), position), (shards_of,), jnp.float32, smallest / len(cuts), high / len(cuts))
        gain = gain * jnp.repeat(jnp.exp(heights), extent[position] // shards_of).reshape((-1,) + (1,) * (len(extent) - 1 - position))
    return gain


def centred(stream_key, dims, spread, most, pieces=(), kind=jnp.bfloat16):
    values = spread * jax.random.normal(stream_key, dims, jnp.float32)
    if pieces:
        values = values * block_levels(stream_key, dims, pieces, -0.22, 0.18)
    return jnp.clip(values, -most, most).astype(kind)


def setup_inputs(seed: int = 0) -> dict:
    key_list = jax.random.split(jax.random.key(seed), 5)
    return {
        "queries": draw_queries(jax.random.fold_in(key_list[4], 71), 0),
        "keys": draw_keys(jax.random.fold_in(key_list[4], 71), 0),
        "values": centred(key_list[2], (SEQ, KV_HEADS * HEAD_DIM), 1.0, 6.0, ((0, 64), (1, 4))),
        "out_weight": centred(key_list[3], (HEADS * HEAD_DIM, D), HEAD_DIM ** -0.5, 0.5, ((0, 4),)),
    }


def reference(queries, keys, values, out_weight):
    group_size = HEADS // KV_HEADS
    score_scale = 1.0 / math.sqrt(HEAD_DIM)
    q_heads = queries.reshape(SEQ, HEADS, HEAD_DIM).transpose(1, 0, 2)
    k_heads = jnp.repeat(keys.reshape(SEQ, KV_HEADS, HEAD_DIM).transpose(1, 0, 2), group_size, axis=0)
    v_heads = jnp.repeat(values.reshape(SEQ, KV_HEADS, HEAD_DIM).transpose(1, 0, 2), group_size, axis=0)
    positions = jnp.arange(SEQ, dtype=jnp.int32)

    def one_head(items):
        q_head, k_head, v_head = items
        q_blocks = q_head.reshape(SEQ // TOK_DEV, TOK_DEV, HEAD_DIM)

        def one_block(entry):
            q_block, number = entry
            scores = jnp.dot(q_block, k_head.T, preferred_element_type=jnp.float32) * score_scale
            row_pos = number * TOK_DEV + jnp.arange(TOK_DEV, dtype=jnp.int32)
            scores = jnp.where(positions[None, :] <= row_pos[:, None], scores, -jnp.inf)
            top_score = lax.optimization_barrier(jnp.max(scores, axis=1, keepdims=True))
            weights = jnp.exp(scores - top_score)
            totals = lax.optimization_barrier(jnp.sum(weights, axis=1, keepdims=True))
            numer = jnp.dot(weights.astype(jnp.bfloat16), v_head, preferred_element_type=jnp.float32)
            return (numer / totals).astype(jnp.bfloat16)
        numbers = jnp.arange(SEQ // TOK_DEV, dtype=jnp.int32)
        return lax.map(one_block, (q_blocks, numbers)).reshape(SEQ, HEAD_DIM)
    attended = lax.map(one_head, (q_heads, k_heads, v_heads))
    attended = attended.transpose(1, 0, 2).reshape(SEQ, HEADS * HEAD_DIM)
    return jnp.dot(attended, out_weight, preferred_element_type=jnp.float32).astype(jnp.bfloat16)
```

```python
import functools
import math

import jax
import jax.numpy as jnp
from jax import lax
from jax.experimental import pallas as pl
from jax.experimental.pallas import tpu as pltpu
from jax.sharding import PartitionSpec as P

HEAD_DIM = 128
GROUP = 4
TOK = 192
UNIT = 2 * TOK
NX, NZ, NY, NC = 4, 2, 4, 2
NHEAD = 4
COLS = 1024
EXP_SCALE = math.log2(math.e) / math.sqrt(HEAD_DIM)
LOW = -1e30
BF16 = jnp.bfloat16
F32 = jnp.float32


def seq_of(x, z, y, c):
    return ((x % NX * NZ + z) * NY + y % NY) * NC + c


def seq_perm(move):
    pairs = []
    for x in range(NX):
        for z in range(NZ):
            for y in range(NY):
                for c in range(NC):
                    pairs.append((seq_of(x, z, y, c), seq_of(*move(x, z, y, c))))
    return pairs


def shift_first(data, d):
    move = lambda x, z, y, c: (x, z, y + d, c) if c == 0 else (x + d, z, y, c)
    return lax.ppermute(data, "seq", seq_perm(move))


def shift_second(data, d):
    move = lambda x, z, y, c: (x + d, z, y, c) if c == 0 else (x, z, y + d, c)
    return lax.ppermute(data, "seq", seq_perm(move))


def swap(data, dz, dc):
    move = lambda x, z, y, c: (x, z ^ dz, y, c ^ dc)
    return lax.ppermute(data, "seq", seq_perm(move))


def place():
    index = lax.axis_index("seq")
    core = lax.rem(index, NC)
    y = lax.rem(index // NC, NY)
    z = lax.rem(index // (NC * NY), NZ)
    x = index // (NC * NY * NZ)
    return x, z, y, core


def order_of(unit):
    first, second, dz = unit
    x, z, y, core = place()
    dx = jnp.where(core == 0, second, first)
    dy = jnp.where(core == 0, first, second)
    zz = 1 - z if dz else z
    return lax.rem(x + dx + NX, NX) * (NZ * NY) + zz * NY + lax.rem(y + dy + NY, NY)


def update(q_ref, max_ref, acc_ref, key, value, mask=None):
    ones = jnp.ones(value.shape, BF16)
    value = jnp.concatenate([value, ones], axis=1)
    for head in range(GROUP):
        rows = pl.ds(head * UNIT, UNIT)
        q = q_ref[:, head * HEAD_DIM : (head + 1) * HEAD_DIM]
        scores = lax.dot_general(
            q, key, (((1,), (1,)), ((), ())), preferred_element_type=F32
        )
        if mask is not None:
            scores = jnp.where(mask, scores, LOW)
        top = jnp.max(scores, axis=1, keepdims=True) * EXP_SCALE
        if mask is None:
            old = max_ref[rows, :1]
            top = jnp.maximum(old, top)
        weights = jnp.exp2(scores * EXP_SCALE - top).astype(BF16)
        product = jnp.dot(weights, value, preferred_element_type=F32)
        if mask is None:
            product += acc_ref[rows, :] * jnp.exp2(old - top)
        acc_ref[rows, :] = product
        max_ref[rows, :] = jnp.broadcast_to(top, (UNIT, HEAD_DIM))


def finish(acc_ref, out_ref):
    for head in range(GROUP):
        rows = pl.ds(head * UNIT, UNIT)
        out_ref[:, head * HEAD_DIM : (head + 1) * HEAD_DIM] = (
            acc_ref[rows, :HEAD_DIM] / acc_ref[rows, HEAD_DIM:]
        ).astype(BF16)


def own_kernel(q_ref, kv_ref, max_ref, acc_ref):
    _, _, _, core = place()
    row = lax.broadcasted_iota(jnp.int32, (UNIT, UNIT), 0)
    col = lax.broadcasted_iota(jnp.int32, (UNIT, UNIT), 1)
    shift = jnp.where(core == 0, 0, TOK)
    row_pos = jnp.where(row < TOK, row + shift, row - shift)
    col_pos = jnp.where(col < TOK, col + shift, col - shift)
    update(
        q_ref,
        max_ref,
        acc_ref,
        kv_ref[:, :HEAD_DIM],
        kv_ref[:, HEAD_DIM:],
        col_pos <= row_pos,
    )


def more_kernel(pieces, last, q_ref, max_in, acc_in, *refs):
    kv_refs = refs[: len(pieces)]
    if last:
        out_ref, max_ref, acc_ref, chosen = refs[len(pieces) :]
    else:
        max_ref, acc_ref, chosen = refs[len(pieces) :]
    max_ref[...] = max_in[...]
    acc_ref[...] = acc_in[...]
    mine = order_of((0, 0, 0))

    for units, kv_ref in zip(pieces, kv_refs):
        count = jnp.int32(0)
        for number, unit in enumerate(units):
            chosen[count] = number
            count = count + (order_of(unit) < mine).astype(jnp.int32)

        def part(place_in_list, kv_ref=kv_ref):
            start = pl.multiple_of(chosen[place_in_list] * UNIT, UNIT)
            block = kv_ref[pl.ds(start, UNIT), :]
            return block[:, :HEAD_DIM], block[:, HEAD_DIM:]

        @pl.loop(0, count // 2)
        def _(pair, part=part):
            key_0, value_0 = part(2 * pair)
            key_1, value_1 = part(2 * pair + 1)
            update(
                q_ref,
                max_ref,
                acc_ref,
                jnp.concatenate([key_0, key_1], axis=0),
                jnp.concatenate([value_0, value_1], axis=0),
            )

        @pl.when(lax.rem(count, 2) == 1)
        def _(part=part, count=count):
            update(q_ref, max_ref, acc_ref, *part(count - 1))

    if last:
        finish(acc_ref, out_ref)


STATE = (
    jax.ShapeDtypeStruct((GROUP * UNIT, HEAD_DIM), F32),
    jax.ShapeDtypeStruct((GROUP * UNIT, 2 * HEAD_DIM), F32),
)
VMEM = pl.BlockSpec(memory_space=pltpu.VMEM)


def cost(units):
    work = GROUP * UNIT * UNIT * units
    return pl.CostEstimate(
        flops=6 * work * HEAD_DIM, bytes_accessed=UNIT * 512 * units, transcendentals=work
    )


def attend_own(q, unit):
    return pl.pallas_call(
        own_kernel,
        out_shape=STATE,
        in_specs=[VMEM] * 2,
        out_specs=(VMEM, VMEM),
        compiler_params=pltpu.CompilerParams(vmem_limit_bytes=40 * 2**20),
        cost_estimate=cost(1),
        name="own",
    )(q, unit)


def attend_more(q, state, pieces, last=False):
    units = [u for u, _ in pieces]
    data = [d for _, d in pieces]
    scratch = [pltpu.SMEM((8,), jnp.int32)]
    if last:
        out_shape = jax.ShapeDtypeStruct((UNIT, GROUP * HEAD_DIM), BF16)
        out_specs = VMEM
        scratch = [pltpu.VMEM(s.shape, s.dtype) for s in STATE] + scratch
    else:
        out_shape = STATE
        out_specs = (VMEM, VMEM)
    return pl.pallas_call(
        functools.partial(more_kernel, units, last),
        out_shape=out_shape,
        in_specs=[VMEM] * (3 + len(data)),
        out_specs=out_specs,
        scratch_shapes=scratch,
        compiler_params=pltpu.CompilerParams(vmem_limit_bytes=40 * 2**20),
        cost_estimate=cost(sum(len(u) for u in units)),
        name="more",
    )(q, *state, *data)


def gather_plane(unit, dz):
    before = shift_first(unit, 1)
    after = shift_first(unit, -1)
    side_before = shift_second(unit, 1)
    side_after = shift_second(unit, -1)
    across = (
        shift_first(before[:TOK], 1),
        shift_first(after[TOK:], -1),
    )
    far_own = shift_second(side_before, 1)
    line = jnp.concatenate([before, after, *across], axis=0)
    line_before = shift_second(line, 1)
    line_after = shift_second(line, -1)
    far_before = shift_second(line_before[:UNIT], 1)
    far_after = shift_second(line_after[UNIT:], -1)
    offsets = (-1, 1, 2)
    return [
        (((0, 0, dz),), unit),
        (tuple((o, 0, dz) for o in offsets), line),
        (((0, -1, dz),), side_before),
        (((0, 1, dz),), side_after),
        (((0, 2, dz),), far_own),
        (tuple((o, -1, dz) for o in offsets), line_before),
        (tuple((o, 1, dz) for o in offsets), line_after),
        (((-1, 2, dz),), far_before),
        (((1, 2, dz), (2, 2, dz)), far_after),
    ]


def project_kernel(where_ref, mine_ref, other_ref, w_ref, out_ref):
    core = where_ref[1]
    half = GROUP * HEAD_DIM
    first = pl.multiple_of(core * half, half)
    second = pl.multiple_of((1 - core) * half, half)
    total = jnp.dot(mine_ref[...], w_ref[pl.ds(first, half), :], preferred_element_type=F32)
    total += jnp.dot(other_ref[...], w_ref[pl.ds(second, half), :], preferred_element_type=F32)
    out_ref[...] = total.astype(BF16)


def project(where, mine, other, weight):
    depth = weight.shape[0]
    tile = 512
    return pl.pallas_call(
        project_kernel,
        out_shape=jax.ShapeDtypeStruct((TOK, COLS), BF16),
        grid_spec=pltpu.PrefetchScalarGridSpec(
            num_scalar_prefetch=1,
            grid=(COLS // tile,),
            in_specs=[
                pl.BlockSpec((TOK, GROUP * HEAD_DIM), lambda i, s: (0, 0)),
                pl.BlockSpec((TOK, GROUP * HEAD_DIM), lambda i, s: (0, 0)),
                pl.BlockSpec((depth, tile), lambda i, s: (0, s[0] * (COLS // tile) + i)),
            ],
            out_specs=pl.BlockSpec((TOK, tile), lambda i, s: (0, i)),
        ),
        compiler_params=pltpu.CompilerParams(vmem_limit_bytes=24 * 2**20),
        cost_estimate=pl.CostEstimate(
            flops=2 * TOK * depth * COLS, bytes_accessed=2 * depth * COLS, transcendentals=0
        ),
        name="project",
    )(where, mine, other, weight)


def add(*terms):
    total = terms[0].astype(F32)
    for term in terms[1:]:
        total = total + term.astype(F32)
    return total.astype(BF16)


TURNS = ((3, 2, 1, 0), (3, 2, 0, 1), (0, 1, 3, 2), (0, 1, 2, 3))


def project_and_sum(mine, other, weight):
    head = lax.axis_index("head")
    core = lax.rem(lax.axis_index("seq"), NC)
    turns = jnp.array(TURNS, jnp.int32)[head]
    chunks = []
    for turn in range(NHEAD):
        where = jnp.stack([turns[turn], core])
        chunks.append(project(where, mine, other, weight))
    ends = lambda data: lax.ppermute(data, "head", [(3, 2), (0, 1)])
    middle = lambda data: lax.ppermute(data, "head", [(2, 1), (1, 2)])
    out = lambda data: lax.ppermute(data, "head", [(1, 0), (2, 3)])
    results = []
    parts = 2
    rows = TOK // parts
    for part in range(parts):
        s = [c[part * rows : (part + 1) * rows] for c in chunks]
        from_end = [ends(c) for c in s[:3]]
        first = middle(add(s[0], from_end[0]))
        second = middle(add(s[1], from_end[1]))
        third = out(add(s[2], first))
        results.append(add(s[3], from_end[2], second, third))
    return jnp.concatenate(results, axis=0)


def halves(array, core):
    width = array.shape[1] // 2
    mine = lax.dynamic_slice_in_dim(array, core * width, width, axis=1)
    other = lax.dynamic_slice_in_dim(array, (1 - core) * width, width, axis=1)
    return mine, other


def local(queries, keys, values, out_weight):
    core = lax.rem(lax.axis_index("seq"), NC)
    k_mine, k_other = halves(keys, core)
    v_mine, v_other = halves(values, core)
    q_mine, q_other = halves(queries, core)
    kv_mine = jnp.concatenate([k_mine, v_mine], axis=1)
    kv_other = jnp.concatenate([k_other, v_other], axis=1)
    unit = jnp.concatenate([kv_mine, swap(kv_other, 0, 1)], axis=0)
    far_unit = jnp.concatenate([swap(kv_mine, 1, 0), swap(kv_other, 1, 1)], axis=0)
    q = jnp.concatenate([q_mine, swap(q_other, 0, 1)], axis=0)

    near = gather_plane(unit, 0)
    far = gather_plane(far_unit, 1)
    state = attend_own(q, unit)
    state = attend_more(q, state, near[1:4] + far[:1])
    state = attend_more(q, state, near[4:7])
    state = attend_more(q, state, near[7:] + far[1:4])
    state = attend_more(q, state, far[4:7])
    attended = attend_more(q, state, far[7:], last=True)

    other = swap(attended[TOK:], 0, 1)
    return project_and_sum(attended[:TOK], other, out_weight)


def solution(mesh):
    placed = (P("seq", "head"), P("seq", "head"), P("seq", "head"), P("head", None))
    return jax.shard_map(
        local, mesh=mesh, in_specs=placed, out_specs=P("seq", "head"), check_vma=False
    )
```

```python
import functools
import math

import jax
import jax.numpy as jnp
from jax import lax
from jax.experimental import pallas as pl
from jax.experimental.pallas import tpu as pltpu
from jax.sharding import PartitionSpec as P

HEAD_DIM = 128
GROUP = 4
TOK = 192
UNIT = 2 * TOK
NX, NZ, NY, NC = 4, 2, 4, 2
NHEAD = 4
COLS = 1024
EXP_SCALE = math.log2(math.e) / math.sqrt(HEAD_DIM)
LOW = -1e30
BF16 = jnp.bfloat16
F32 = jnp.float32


def seq_of(x, z, y, c):
    return ((x % NX * NZ + z) * NY + y % NY) * NC + c


def seq_perm(move):
    pairs = []
    for x in range(NX):
        for z in range(NZ):
            for y in range(NY):
                for c in range(NC):
                    pairs.append((seq_of(x, z, y, c), seq_of(*move(x, z, y, c))))
    return pairs


def shift_first(data, d):
    move = lambda x, z, y, c: (x, z, y + d, c) if c == 0 else (x + d, z, y, c)
    return lax.ppermute(data, "seq", seq_perm(move))


def shift_second(data, d):
    move = lambda x, z, y, c: (x + d, z, y, c) if c == 0 else (x, z, y + d, c)
    return lax.ppermute(data, "seq", seq_perm(move))


def swap(data, dz, dc):
    move = lambda x, z, y, c: (x, z ^ dz, y, c ^ dc)
    return lax.ppermute(data, "seq", seq_perm(move))


def place():
    index = lax.axis_index("seq")
    core = lax.rem(index, NC)
    y = lax.rem(index // NC, NY)
    z = lax.rem(index // (NC * NY), NZ)
    x = index // (NC * NY * NZ)
    return x, z, y, core


def order_of(unit):
    first, second, dz = unit
    x, z, y, core = place()
    dx = jnp.where(core == 0, second, first)
    dy = jnp.where(core == 0, first, second)
    zz = 1 - z if dz else z
    return lax.rem(x + dx + NX, NX) * (NZ * NY) + zz * NY + lax.rem(y + dy + NY, NY)


HALF = TOK // 2
PARTS = 2
PAIR = 2
TILE = PAIR * TOK
TILES = GROUP // PAIR
LINE = 4
STATE = (
    jax.ShapeDtypeStruct((PARTS * GROUP * TOK, HEAD_DIM), F32),
    jax.ShapeDtypeStruct((PARTS * GROUP * TOK, 2 * HEAD_DIM), F32),
)
VMEM = pl.BlockSpec(memory_space=pltpu.VMEM)
KERNEL_COST = pl.CostEstimate(flops=2**30, bytes_accessed=2**20, transcendentals=2**20)


def tile_of(q_ref, tile):
    heads = range(tile * PAIR, (tile + 1) * PAIR)
    q = [q_ref[:, head * HEAD_DIM : (head + 1) * HEAD_DIM] for head in heads]
    mark = lax.broadcasted_iota(jnp.int32, (TILE, HEAD_DIM), 1) == 0
    return jnp.concatenate([jnp.concatenate(q, axis=0), mark.astype(F32).astype(BF16)], axis=1)


def hidden_keys(kv_ref, allowed):
    columns = [jnp.full((UNIT, HEAD_DIM), jnp.where(a, 0.0, LOW), F32) for a in allowed]
    columns = jnp.concatenate(columns, axis=0).astype(BF16)
    return jnp.concatenate([kv_ref[:, :HEAD_DIM], columns], axis=1)


def own_bias(part):
    _, _, _, core = place()
    shift = jnp.where(core == 0, 0, TOK)
    row = lax.broadcasted_iota(jnp.int32, (TILE, UNIT), 0) % TOK
    col = lax.broadcasted_iota(jnp.int32, (TILE, UNIT), 1)
    row_pos = jnp.where(row < HALF, row + shift, row - HALF + TOK - shift) + part * HALF
    col_pos = jnp.where(col < TOK, col + shift, col - shift)
    return jnp.where(col_pos <= row_pos, 0.0, LOW).astype(F32)


def attend_kernel(lines, parts, first, last, *refs):
    refs = list(refs)
    q_refs = {part: refs.pop(0) for part in parts}
    kv_refs = [refs.pop(0) for _ in lines]
    state_in = None if first else (refs.pop(0), refs.pop(0))
    out_ref = refs.pop(0) if last else None
    state_out = refs
    mine = order_of((0, 0, 0))
    steps = [(line, p, t) for line in range(len(lines)) for p in parts for t in range(TILES)]
    keys, values = {}, {}

    def scores_of(step):
        line, part, tile = step
        if line not in keys:
            allowed = [order_of(unit) < mine for unit in lines[line]]
            if first and line == 0:
                allowed[0] = True
            keys[line] = hidden_keys(kv_refs[line], allowed)
            value = kv_refs[line][:, HEAD_DIM:]
            values[line] = jnp.concatenate([value, jnp.ones(value.shape, BF16)], axis=1)
        q = tile_of(q_refs[part], tile)
        scores = lax.dot_general(
            q, keys[line], (((1,), (1,)), ((), ())), preferred_element_type=F32
        )
        if first and line == 0:
            own = scores[:, :UNIT] + own_bias(part)
            scores = jnp.concatenate([own, scores[:, UNIT:]], axis=1)
        return scores

    ahead = scores_of(steps[0])
    for number, (line, part, tile) in enumerate(steps):
        scores = ahead
        if number + 1 < len(steps):
            ahead = scores_of(steps[number + 1])
        rows = pl.ds((part * TILES + tile) * TILE, TILE)
        state = state_in if line == 0 else state_out
        top = jnp.max(scores, axis=1, keepdims=True) * EXP_SCALE
        if state is not None:
            old = state[0][rows, :1]
            top = jnp.maximum(old, top)
        weights = jnp.exp2(scores * EXP_SCALE - top).astype(BF16)
        product = jnp.dot(weights, values[line], preferred_element_type=F32)
        if state is not None:
            product += state[1][rows, :] * jnp.exp2(old - top)
        if last and line + 1 == len(lines):
            result = (product[:, :HEAD_DIM] / product[:, HEAD_DIM:]).astype(BF16)
            for number_in_tile in range(PAIR):
                head = tile * PAIR + number_in_tile
                out_ref[:, head * HEAD_DIM : (head + 1) * HEAD_DIM] = result[
                    number_in_tile * TOK : (number_in_tile + 1) * TOK
                ]
        else:
            state_out[0][rows, :] = jnp.broadcast_to(top, (TILE, HEAD_DIM))
            state_out[1][rows, :] = product


def attend(q, state, lines, part=None):
    last = part is not None
    parts = (part,) if last else tuple(range(PARTS))
    if last:
        out_shape = jax.ShapeDtypeStruct((TOK, GROUP * HEAD_DIM), BF16)
        out_specs = VMEM
        scratch = [pltpu.VMEM(s.shape, s.dtype) for s in STATE]
    else:
        out_shape = STATE
        out_specs = (VMEM, VMEM)
        scratch = []
    args = [*(q[p] for p in parts), *(data for _, data in lines), *(state or ())]
    return pl.pallas_call(
        functools.partial(attend_kernel, [u for u, _ in lines], parts, state is None, last),
        out_shape=out_shape,
        in_specs=[VMEM] * len(args),
        out_specs=out_specs,
        scratch_shapes=scratch,
        compiler_params=pltpu.CompilerParams(vmem_limit_bytes=24 * 2**20),
        cost_estimate=KERNEL_COST,
        name="attend",
    )(*args)


OFFSETS = (0, -1, 1, 2)


def units_at(second, dz):
    return tuple((first, second, dz) for first in OFFSETS)


def line_of(unit):
    return (unit, shift_first(unit, 1), shift_first(unit, -1), shift_first(unit, 2))


def tie(*arrays):
    return lax.optimization_barrier(arrays)


def project_kernel(turns, where_ref, mine_ref, other_ref, w_ref, *out_refs):
    core = where_ref[NHEAD]
    half = GROUP * HEAD_DIM
    first = pl.multiple_of(core * half, half)
    second = pl.multiple_of((1 - core) * half, half)
    for turn, out_ref in zip(turns, out_refs):
        columns = pl.ds(pl.multiple_of(where_ref[turn] * COLS, COLS), COLS)
        total = jnp.dot(
            mine_ref[...], w_ref[pl.ds(first, half), columns], preferred_element_type=F32
        )
        total += jnp.dot(
            other_ref[...], w_ref[pl.ds(second, half), columns], preferred_element_type=F32
        )
        out_ref[...] = total.astype(BF16)


def project(turns, where, mine, other, weight):
    return pl.pallas_call(
        functools.partial(project_kernel, turns),
        out_shape=[jax.ShapeDtypeStruct((HALF, COLS), BF16)] * len(turns),
        in_specs=[pl.BlockSpec(memory_space=pltpu.SMEM)] + [VMEM] * 3,
        out_specs=[VMEM] * len(turns),
        compiler_params=pltpu.CompilerParams(vmem_limit_bytes=24 * 2**20),
        cost_estimate=KERNEL_COST,
        name="project",
    )(where, mine, other, weight)


def add(*terms):
    total = terms[0].astype(F32)
    for term in terms[1:]:
        total = total + term.astype(F32)
    return total.astype(BF16)


TURNS = ((3, 2, 1, 0), (3, 2, 0, 1), (0, 1, 3, 2), (0, 1, 2, 3))


def turns_and_core():
    head = lax.axis_index("head")
    core = lax.rem(lax.axis_index("seq"), NC)
    table = jnp.array([[*turns, c] for turns in TURNS for c in range(NC)], jnp.int32)
    return lax.dynamic_index_in_dim(table, head * NC + core, 0, keepdims=False)


def outer(data):
    return lax.ppermute(data, "head", [(3, 2), (2, 3), (1, 0), (0, 1)])


def inner(data):
    return lax.ppermute(data, "head", [(2, 1), (1, 2)])


def project_and_sum(where, one, two, weight):
    a = list(project((0,), where, *one, weight))
    outer_0 = outer(a[0])
    where, a[0] = tie(where, a[0])
    a += list(project((1, 2, 3), where, *one, weight))
    outer_1 = outer(a[1])
    where, a[1] = tie(where, a[1])
    b = list(project((0, 1, 2, 3), where, *two, weight))
    sum_0 = add(a[0], outer_0)
    sum_0, b[0] = tie(sum_0, b[0])
    inner_0 = inner(sum_0)
    outer_0b = outer(b[0])
    sum_1 = add(a[1], outer_1)
    sum_1, b[1] = tie(sum_1, b[1])
    inner_1 = inner(sum_1)
    outer_1b = outer(b[1])
    sum_2 = add(a[2], inner_0)
    sum_0b = add(b[0], outer_0b)
    sum_2, sum_0b = tie(sum_2, sum_0b)
    outer_2 = outer(sum_2)
    inner_0b = inner(sum_0b)
    inner_1b = inner(add(b[1], outer_1b))
    outer_2b = outer(add(b[2], inner_0b))
    result_a = add(a[3], outer_2, inner_1)
    result_b = add(b[3], outer_2b, inner_1b)
    return jnp.concatenate([result_a, result_b], axis=0)


def halves(array, core):
    width = array.shape[1] // 2
    mine = lax.dynamic_slice_in_dim(array, core * width, width, axis=1)
    other = lax.dynamic_slice_in_dim(array, (1 - core) * width, width, axis=1)
    return mine, other


def local(queries, keys, values, out_weight):
    core = lax.rem(lax.axis_index("seq"), NC)
    where = turns_and_core()
    k_mine, k_other = halves(keys, core)
    v_mine, v_other = halves(values, core)
    kv_mine = jnp.concatenate([k_mine, v_mine], axis=1)
    kv_other = jnp.concatenate([k_other, v_other], axis=1)
    near_unit = jnp.concatenate([kv_mine, swap(kv_other, 0, 1)], axis=0)
    far_unit = jnp.concatenate([swap(kv_mine, 1, 0), swap(kv_other, 1, 1)], axis=0)

    queries, _ = tie(queries, near_unit)
    q_mine, q_other = halves(queries, core)
    q_got = swap(q_other, 0, 1)
    q = [
        jnp.concatenate([q_mine[part], q_got[part]], axis=0)
        for part in (slice(0, HALF), slice(HALF, TOK))
    ]

    near = jnp.concatenate(line_of(near_unit), axis=0)
    near, far_unit = tie(near, far_unit)
    near_lines = [shift_second(near, d) for d in (1, -1, 2)]
    state = attend(q, None, [(units_at(0, 0), near)])
    far = jnp.concatenate(line_of(far_unit), axis=0)
    far, where, *state = tie(far, where, *state)
    far_lines = [shift_second(far, d) for d in (1, -1, 2)]
    state = attend(q, state, [(units_at(0, 1), far)])
    for second, line in zip((-1, 1, 2), near_lines):
        state = attend(q, state, [(units_at(second, 0), line)])
    for second, line in zip((-1, 1), far_lines):
        state = attend(q, state, [(units_at(second, 1), line)])
    across = [(units_at(2, 1), far_lines[2])]
    one = attend(q, state, across, part=0)
    one_other = swap(one[HALF:], 0, 1)
    q[1], one = tie(q[1], one)
    two = attend(q, state, across, part=1)
    two_other = swap(two[HALF:], 0, 1)
    return project_and_sum(
        where, (one[:HALF], one_other), (two[:HALF], two_other), out_weight
    )


def solution(mesh):
    placed = (P("seq", "head"), P("seq", "head"), P("seq", "head"), P("head", None))
    return jax.shard_map(
        local, mesh=mesh, in_specs=placed, out_specs=P("seq", "head"), check_vma=False
    )
```

```python
import functools
import math

import jax
import jax.numpy as jnp
from jax import lax
from jax.experimental import pallas as pl
from jax.experimental.pallas import tpu as pltpu
from jax.sharding import PartitionSpec as P

HEAD_DIM = 128
GROUP = 4
TOK = 192
UNIT = 2 * TOK
NX, NZ, NY, NC = 4, 2, 4, 2
NHEAD = 4
COLS = 1024
EXP_SCALE = math.log2(math.e) / math.sqrt(HEAD_DIM)
LOW = -1e30
BF16 = jnp.bfloat16
F32 = jnp.float32


def seq_of(x, z, y, c):
    return ((x % NX * NZ + z) * NY + y % NY) * NC + c


def seq_perm(move):
    pairs = []
    for x in range(NX):
        for z in range(NZ):
            for y in range(NY):
                for c in range(NC):
                    pairs.append((seq_of(x, z, y, c), seq_of(*move(x, z, y, c))))
    return pairs


def shift_first(data, d):
    move = lambda x, z, y, c: (x, z, y + d, c) if c == 0 else (x + d, z, y, c)
    return lax.ppermute(data, "seq", seq_perm(move))


def shift_second(data, d):
    move = lambda x, z, y, c: (x + d, z, y, c) if c == 0 else (x, z, y + d, c)
    return lax.ppermute(data, "seq", seq_perm(move))


def swap(data, dz, dc):
    move = lambda x, z, y, c: (x, z ^ dz, y, c ^ dc)
    return lax.ppermute(data, "seq", seq_perm(move))


def place():
    index = lax.axis_index("seq")
    core = lax.rem(index, NC)
    y = lax.rem(index // NC, NY)
    z = lax.rem(index // (NC * NY), NZ)
    x = index // (NC * NY * NZ)
    return x, z, y, core


def order_of(unit):
    first, second, dz = unit
    x, z, y, core = place()
    dx = jnp.where(core == 0, second, first)
    dy = jnp.where(core == 0, first, second)
    zz = 1 - z if dz else z
    return lax.rem(x + dx + NX, NX) * (NZ * NY) + zz * NY + lax.rem(y + dy + NY, NY)


HALF = TOK // 2
LINE = 4
STATE = (
    jax.ShapeDtypeStruct((GROUP * UNIT, HEAD_DIM), F32),
    jax.ShapeDtypeStruct((GROUP * UNIT, 2 * HEAD_DIM), F32),
)
VMEM = pl.BlockSpec(memory_space=pltpu.VMEM)
SHORT = pl.CostEstimate(flops=2**26, bytes_accessed=2**16, transcendentals=2**16)
LONG = pl.CostEstimate(flops=2**31, bytes_accessed=2**20, transcendentals=0)


def hidden_keys(kv_ref, allowed):
    columns = [jnp.full((UNIT, HEAD_DIM), jnp.where(a, 0.0, LOW), F32) for a in allowed]
    columns = jnp.concatenate(columns, axis=0).astype(BF16)
    return jnp.concatenate([kv_ref[:, :HEAD_DIM], columns], axis=1)


def own_bias():
    _, _, _, core = place()
    row = lax.broadcasted_iota(jnp.int32, (UNIT, UNIT), 0)
    col = lax.broadcasted_iota(jnp.int32, (UNIT, UNIT), 1)
    shift = jnp.where(core == 0, 0, TOK)
    row_pos = jnp.where(row < TOK, row + shift, row - shift)
    col_pos = jnp.where(col < TOK, col + shift, col - shift)
    return jnp.where(col_pos <= row_pos, 0.0, LOW).astype(F32)


def attend_kernel(lines, first, last, q_ref, *refs):
    refs = list(refs)
    kv_refs = [refs.pop(0) for _ in lines]
    state_in = None if first else (refs.pop(0), refs.pop(0))
    out_ref = refs.pop(0) if last else None
    state_out = refs
    mine = order_of((0, 0, 0))
    mark = lax.broadcasted_iota(jnp.int32, (UNIT, HEAD_DIM), 1) == 0
    mark = mark.astype(F32).astype(BF16)
    steps = [(line, head) for line in range(len(lines)) for head in range(GROUP)]
    keys, values = {}, {}

    def scores_of(step):
        line, head = step
        if line not in keys:
            allowed = [order_of(unit) < mine for unit in lines[line]]
            if first and line == 0:
                allowed[0] = True
            keys[line] = hidden_keys(kv_refs[line], allowed)
            value = kv_refs[line][:, HEAD_DIM:]
            values[line] = jnp.concatenate([value, jnp.ones(value.shape, BF16)], axis=1)
        q = q_ref[:, head * HEAD_DIM : (head + 1) * HEAD_DIM]
        scores = lax.dot_general(
            jnp.concatenate([q, mark], axis=1),
            keys[line],
            (((1,), (1,)), ((), ())),
            preferred_element_type=F32,
        )
        if first and line == 0:
            own = scores[:, :UNIT] + own_bias()
            scores = jnp.concatenate([own, scores[:, UNIT:]], axis=1)
        return scores

    ahead = scores_of(steps[0])
    for number, (line, head) in enumerate(steps):
        scores = ahead
        if number + 1 < len(steps):
            ahead = scores_of(steps[number + 1])
        rows = pl.ds(head * UNIT, UNIT)
        state = state_in if line == 0 else state_out
        top = jnp.max(scores, axis=1, keepdims=True) * EXP_SCALE
        if state is not None:
            old = state[0][rows, :1]
            top = jnp.maximum(old, top)
        weights = jnp.exp2(scores * EXP_SCALE - top).astype(BF16)
        product = jnp.dot(weights, values[line], preferred_element_type=F32)
        if state is not None:
            product += state[1][rows, :] * jnp.exp2(old - top)
        if last and line + 1 == len(lines):
            result = product[:, :HEAD_DIM] / product[:, HEAD_DIM:]
            out_ref[:, head * HEAD_DIM : (head + 1) * HEAD_DIM] = result.astype(BF16)
        else:
            state_out[0][rows, :] = jnp.broadcast_to(top, (UNIT, HEAD_DIM))
            state_out[1][rows, :] = product


def attend(q, state, lines, last=False):
    if last:
        out_shape = jax.ShapeDtypeStruct((UNIT, GROUP * HEAD_DIM), BF16)
        out_specs = VMEM
        scratch = [pltpu.VMEM(s.shape, s.dtype) for s in STATE]
    else:
        out_shape = STATE
        out_specs = (VMEM, VMEM)
        scratch = []
    args = [q, *(data for _, data in lines), *(state or ())]
    return pl.pallas_call(
        functools.partial(attend_kernel, [u for u, _ in lines], state is None, last),
        out_shape=out_shape,
        in_specs=[VMEM] * len(args),
        out_specs=out_specs,
        scratch_shapes=scratch,
        compiler_params=pltpu.CompilerParams(vmem_limit_bytes=24 * 2**20),
        cost_estimate=SHORT,
        name="attend",
    )(*args)


OFFSETS = (0, -1, 1, 2)


def units_at(second, dz):
    return tuple((first, second, dz) for first in OFFSETS)


def line_of(unit):
    return (unit, shift_first(unit, 1), shift_first(unit, -1), shift_first(unit, 2))


def tie(*arrays):
    return lax.optimization_barrier(arrays)


def after(array, earlier):
    return tie(array, earlier)[0]


def project_kernel(turns, where_ref, mine_ref, other_ref, w_ref, *out_refs):
    core = where_ref[NHEAD]
    half = GROUP * HEAD_DIM
    first = pl.multiple_of(core * half, half)
    second = pl.multiple_of((1 - core) * half, half)
    for number, turn in enumerate(turns):
        columns = pl.ds(pl.multiple_of(where_ref[turn] * COLS, COLS), COLS)
        total = jnp.dot(
            mine_ref[...], w_ref[pl.ds(first, half), columns], preferred_element_type=F32
        )
        total += jnp.dot(
            other_ref[...], w_ref[pl.ds(second, half), columns], preferred_element_type=F32
        )
        total = total.astype(BF16)
        out_refs[2 * number][...] = total[:HALF]
        out_refs[2 * number + 1][...] = total[HALF:]


def project(turns, where, mine, other, weight):
    count = 2 * len(turns)
    return pl.pallas_call(
        functools.partial(project_kernel, turns),
        out_shape=[jax.ShapeDtypeStruct((HALF, COLS), BF16)] * count,
        in_specs=[pl.BlockSpec(memory_space=pltpu.SMEM)] + [VMEM] * 3,
        out_specs=[VMEM] * count,
        compiler_params=pltpu.CompilerParams(vmem_limit_bytes=24 * 2**20),
        cost_estimate=LONG,
        name="project",
    )(where, mine, other, weight)


def add(*terms):
    total = terms[0].astype(F32)
    for term in terms[1:]:
        total = total + term.astype(F32)
    return total.astype(BF16)


TURNS = ((3, 2, 1, 0), (3, 2, 0, 1), (0, 1, 3, 2), (0, 1, 2, 3))


def turns_and_core():
    head = lax.axis_index("head")
    core = lax.rem(lax.axis_index("seq"), NC)
    table = jnp.array([[*turns, c] for turns in TURNS for c in range(NC)], jnp.int32)
    return lax.dynamic_index_in_dim(table, head * NC + core, 0, keepdims=False)


def outer(data):
    return lax.ppermute(data, "head", [(3, 2), (2, 3), (1, 0), (0, 1)])


def inner(data):
    return lax.ppermute(data, "head", [(2, 1), (1, 2)])


def project_and_sum(where, mine, other, weight):
    a_0, b_0 = project((0,), where, mine, other, weight)
    outer_0a, outer_0b = outer(a_0), outer(b_0)
    where, a_0 = tie(where, a_0)
    a_1, b_1, a_2, b_2, a_3, b_3 = project((1, 2, 3), where, mine, other, weight)
    outer_1a, outer_1b = outer(a_1), outer(b_1)
    sum_0a, sum_0b = add(a_0, outer_0a), add(b_0, outer_0b)
    sum_0a, a_1, b_1 = tie(sum_0a, a_1, b_1)
    inner_0a = inner(sum_0a)
    inner_0b = inner(after(sum_0b, sum_0a))
    sum_1a = after(add(a_1, outer_1a), sum_0b)
    inner_1a = inner(sum_1a)
    sum_2a = add(a_2, inner_0a)
    outer_2a = outer(sum_2a)
    sum_1b = after(add(b_1, outer_1b), sum_2a)
    inner_1b = inner(sum_1b)
    outer_2b = outer(add(b_2, inner_0b))
    result_a = add(a_3, outer_2a, inner_1a)
    result_b = add(b_3, outer_2b, inner_1b)
    return jnp.concatenate([result_a, result_b], axis=0)


def halves(array, core):
    width = array.shape[1] // 2
    mine = lax.dynamic_slice_in_dim(array, core * width, width, axis=1)
    other = lax.dynamic_slice_in_dim(array, (1 - core) * width, width, axis=1)
    return mine, other


def local(queries, keys, values, out_weight):
    core = lax.rem(lax.axis_index("seq"), NC)
    where = turns_and_core()
    k_mine, k_other = halves(keys, core)
    v_mine, v_other = halves(values, core)
    kv_mine = jnp.concatenate([k_mine, v_mine], axis=1)
    kv_other = jnp.concatenate([k_other, v_other], axis=1)
    near_unit = jnp.concatenate([kv_mine, swap(kv_other, 0, 1)], axis=0)
    far_unit = jnp.concatenate([swap(kv_mine, 1, 0), swap(kv_other, 1, 1)], axis=0)

    queries, _ = tie(queries, near_unit)
    q_mine, q_other = halves(queries, core)
    q_got = swap(q_other, 0, 1)
    q = jnp.concatenate([q_mine, q_got], axis=0)

    near = jnp.concatenate(line_of(near_unit), axis=0)
    near, far_unit = tie(near, far_unit)
    near_before, near_after = shift_second(near, 1), shift_second(near, -1)
    state = attend(q, None, [(units_at(0, 0), near)])
    far = jnp.concatenate(line_of(far_unit), axis=0)
    far, where, *state = tie(far, where, *state)
    far_before, far_after = shift_second(far, 1), shift_second(far, -1)
    state = attend(q, state, [(units_at(0, 1), far)])
    near_before, near_after, *state = tie(near_before, near_after, *state)
    half = UNIT * LINE // 2
    near_across = jnp.concatenate(
        [shift_second(near_before[:half], 1), shift_second(near_after[half:], -1)], axis=0
    )
    state = attend(q, state, [(units_at(-1, 0), near_before)])
    state = attend(q, state, [(units_at(1, 0), near_after)])
    far_before, far_after, *state = tie(far_before, far_after, *state)
    far_across = jnp.concatenate(
        [shift_second(far_before[:half], 1), shift_second(far_after[half:], -1)], axis=0
    )
    state = attend(q, state, [(units_at(-1, 1), far_before)])
    state = attend(q, state, [(units_at(1, 1), far_after)])
    state = attend(q, state, [(units_at(2, 0), near_across)])
    attended = attend(q, state, [(units_at(2, 1), far_across)], last=True)
    other = swap(attended[TOK:], 0, 1)
    return project_and_sum(where, attended[:TOK], other, out_weight)


def solution(mesh):
    placed = (P("seq", "head"), P("seq", "head"), P("seq", "head"), P("head", None))
    return jax.shard_map(
        local, mesh=mesh, in_specs=placed, out_specs=P("seq", "head"), check_vma=False
    )
```

```python
import functools
import math

import jax
import jax.numpy as jnp
from jax import lax
from jax.experimental import pallas as pl
from jax.experimental.pallas import tpu as pltpu
from jax.sharding import PartitionSpec as P

HEAD_DIM = 128
GROUP = 4
TOK = 192
UNIT = 2 * TOK
NX, NZ, NY, NC = 4, 2, 4, 2
NHEAD = 4
COLS = 1024
EXP_SCALE = math.log2(math.e) / math.sqrt(HEAD_DIM)
LOW = -1e30
BF16 = jnp.bfloat16
F32 = jnp.float32


def seq_of(x, z, y, c):
    return ((x % NX * NZ + z) * NY + y % NY) * NC + c


def seq_perm(move):
    pairs = []
    for x in range(NX):
        for z in range(NZ):
            for y in range(NY):
                for c in range(NC):
                    pairs.append((seq_of(x, z, y, c), seq_of(*move(x, z, y, c))))
    return pairs


def partner(place, d):
    return place + (d if place % 2 == 0 else -d)


def pair_first(data, d):
    move = lambda x, z, y, c: (x, z, partner(y, d), c) if c == 0 else (partner(x, d), z, y, c)
    return lax.ppermute(data, "seq", seq_perm(move))


def pair_second(data, d):
    move = lambda x, z, y, c: (partner(x, d), z, y, c) if c == 0 else (x, z, partner(y, d), c)
    return lax.ppermute(data, "seq", seq_perm(move))


def swap(data, dz, dc):
    move = lambda x, z, y, c: (x, z ^ dz, y, c ^ dc)
    return lax.ppermute(data, "seq", seq_perm(move))


def place():
    index = lax.axis_index("seq")
    core = lax.rem(index, NC)
    y = lax.rem(index // NC, NY)
    z = lax.rem(index // (NC * NY), NZ)
    x = index // (NC * NY * NZ)
    return x, z, y, core


def order_of(unit):
    first, second, dz = unit
    x, z, y, core = place()
    dx = jnp.where(core == 0, second, first) * (1 - 2 * lax.rem(x, 2))
    dy = jnp.where(core == 0, first, second) * (1 - 2 * lax.rem(y, 2))
    zz = 1 - z if dz else z
    return lax.rem(x + dx + NX, NX) * (NZ * NY) + zz * NY + lax.rem(y + dy + NY, NY)


HALF = TOK // 2
LINE = 4
STATE = (
    jax.ShapeDtypeStruct((GROUP * UNIT, HEAD_DIM), F32),
    jax.ShapeDtypeStruct((GROUP * UNIT, 2 * HEAD_DIM), F32),
)
VMEM = pl.BlockSpec(memory_space=pltpu.VMEM)
SHORT = pl.CostEstimate(flops=2**26, bytes_accessed=2**16, transcendentals=2**16)
LONG = pl.CostEstimate(flops=2**31, bytes_accessed=2**20, transcendentals=0)


def hidden_keys(kv_ref, allowed):
    columns = [jnp.full((UNIT, HEAD_DIM), jnp.where(a, 0.0, LOW), F32) for a in allowed]
    columns = jnp.concatenate(columns, axis=0).astype(BF16)
    return jnp.concatenate([kv_ref[:, :HEAD_DIM], columns], axis=1)


def own_bias():
    _, _, _, core = place()
    row = lax.broadcasted_iota(jnp.int32, (UNIT, UNIT), 0)
    col = lax.broadcasted_iota(jnp.int32, (UNIT, UNIT), 1)
    shift = jnp.where(core == 0, 0, TOK)
    row_pos = jnp.where(row < TOK, row + shift, row - shift)
    col_pos = jnp.where(col < TOK, col + shift, col - shift)
    return jnp.where(col_pos <= row_pos, 0.0, LOW).astype(F32)


def attend_kernel(lines, first, last, q_ref, *refs):
    refs = list(refs)
    kv_refs = [refs.pop(0) for _ in lines]
    state_in = None if first else (refs.pop(0), refs.pop(0))
    out_ref = refs.pop(0) if last else None
    state_out = refs
    mine = order_of((0, 0, 0))
    mark = lax.broadcasted_iota(jnp.int32, (UNIT, HEAD_DIM), 1) == 0
    mark = mark.astype(F32).astype(BF16)
    steps = [(line, head) for line in range(len(lines)) for head in range(GROUP)]
    keys, values = {}, {}

    def scores_of(step):
        line, head = step
        if line not in keys:
            allowed = [order_of(unit) < mine for unit in lines[line]]
            if first and line == 0:
                allowed[0] = True
            keys[line] = hidden_keys(kv_refs[line], allowed)
            value = kv_refs[line][:, HEAD_DIM:]
            values[line] = jnp.concatenate([value, jnp.ones(value.shape, BF16)], axis=1)
        q = q_ref[:, head * HEAD_DIM : (head + 1) * HEAD_DIM]
        scores = lax.dot_general(
            jnp.concatenate([q, mark], axis=1),
            keys[line],
            (((1,), (1,)), ((), ())),
            preferred_element_type=F32,
        )
        if first and line == 0:
            own = scores[:, :UNIT] + own_bias()
            scores = jnp.concatenate([own, scores[:, UNIT:]], axis=1)
        return scores

    ahead = scores_of(steps[0])
    for number, (line, head) in enumerate(steps):
        scores = ahead
        if number + 1 < len(steps):
            ahead = scores_of(steps[number + 1])
        rows = pl.ds(head * UNIT, UNIT)
        state = state_in if line == 0 else state_out
        top = jnp.max(scores, axis=1, keepdims=True) * EXP_SCALE
        if state is not None:
            old = state[0][rows, :1]
            top = jnp.maximum(old, top)
        weights = jnp.exp2(scores * EXP_SCALE - top).astype(BF16)
        product = jnp.dot(weights, values[line], preferred_element_type=F32)
        if state is not None:
            product += state[1][rows, :] * jnp.exp2(old - top)
        if last and line + 1 == len(lines):
            result = product[:, :HEAD_DIM] / product[:, HEAD_DIM:]
            out_ref[:, head * HEAD_DIM : (head + 1) * HEAD_DIM] = result.astype(BF16)
        else:
            state_out[0][rows, :] = jnp.broadcast_to(top, (UNIT, HEAD_DIM))
            state_out[1][rows, :] = product


def attend(q, state, lines, last=False):
    if last:
        out_shape = jax.ShapeDtypeStruct((UNIT, GROUP * HEAD_DIM), BF16)
        out_specs = VMEM
        scratch = [pltpu.VMEM(s.shape, s.dtype) for s in STATE]
    else:
        out_shape = STATE
        out_specs = (VMEM, VMEM)
        scratch = []
    args = [q, *(data for _, data in lines), *(state or ())]
    return pl.pallas_call(
        functools.partial(attend_kernel, [u for u, _ in lines], state is None, last),
        out_shape=out_shape,
        in_specs=[VMEM] * len(args),
        out_specs=out_specs,
        scratch_shapes=scratch,
        compiler_params=pltpu.CompilerParams(vmem_limit_bytes=24 * 2**20),
        cost_estimate=SHORT,
        name="attend",
    )(*args)


OFFSETS = (0, 1, -1, 2)


def units_at(second, dz):
    return tuple((first, second, dz) for first in OFFSETS)


def line_of(unit):
    return (unit, pair_first(unit, 1), pair_first(unit, -1), pair_first(unit, 2))


def tie(*arrays):
    return lax.optimization_barrier(arrays)


def after(array, earlier):
    return tie(array, earlier)[0]


def chunk_of(turn):
    head = lax.axis_index("head")
    chunk = jnp.int32(TURNS[0][turn])
    for number in range(1, NHEAD):
        chunk = jnp.where(head == number, TURNS[number][turn], chunk)
    return chunk


def project_kernel(turns, mine_ref, other_ref, w_ref, *out_refs):
    _, _, _, core = place()
    half = GROUP * HEAD_DIM
    first = pl.multiple_of(core * half, half)
    second = pl.multiple_of((1 - core) * half, half)
    for number, turn in enumerate(turns):
        columns = pl.ds(pl.multiple_of(chunk_of(turn) * COLS, COLS), COLS)
        total = jnp.dot(
            mine_ref[...], w_ref[pl.ds(first, half), columns], preferred_element_type=F32
        )
        total += jnp.dot(
            other_ref[...], w_ref[pl.ds(second, half), columns], preferred_element_type=F32
        )
        total = total.astype(BF16)
        out_refs[2 * number][...] = total[:HALF]
        out_refs[2 * number + 1][...] = total[HALF:]


def project(turns, mine, other, weight):
    count = 2 * len(turns)
    return pl.pallas_call(
        functools.partial(project_kernel, turns),
        out_shape=[jax.ShapeDtypeStruct((HALF, COLS), BF16)] * count,
        in_specs=[VMEM] * 3,
        out_specs=[VMEM] * count,
        compiler_params=pltpu.CompilerParams(vmem_limit_bytes=24 * 2**20),
        cost_estimate=LONG,
        name="project",
    )(mine, other, weight)


def add(*terms):
    total = terms[0].astype(F32)
    for term in terms[1:]:
        total = total + term.astype(F32)
    return total.astype(BF16)


TURNS = ((3, 2, 1, 0), (3, 2, 0, 1), (0, 1, 3, 2), (0, 1, 2, 3))


def outer(data):
    return lax.ppermute(data, "head", [(3, 2), (2, 3), (1, 0), (0, 1)])


def inner(data):
    return lax.ppermute(data, "head", [(2, 1), (1, 2)])


def project_and_sum(mine, other, weight):
    a_0, b_0 = project((0,), mine, other, weight)
    outer_0a, outer_0b = outer(a_0), outer(b_0)
    mine, a_0 = tie(mine, a_0)
    a_1, b_1, a_2, b_2, a_3, b_3 = project((1, 2, 3), mine, other, weight)
    outer_1a, outer_1b = outer(a_1), outer(b_1)
    sum_0a, sum_0b = add(a_0, outer_0a), add(b_0, outer_0b)
    sum_0a, a_1, b_1 = tie(sum_0a, a_1, b_1)
    inner_0a = inner(sum_0a)
    inner_0b = inner(after(sum_0b, sum_0a))
    sum_1a = after(add(a_1, outer_1a), sum_0b)
    inner_1a = inner(sum_1a)
    sum_2a = add(a_2, inner_0a)
    outer_2a = outer(sum_2a)
    sum_1b = after(add(b_1, outer_1b), sum_2a)
    inner_1b = inner(sum_1b)
    outer_2b = outer(add(b_2, inner_0b))
    result_a = add(a_3, outer_2a, inner_1a)
    result_b = add(b_3, outer_2b, inner_1b)
    return jnp.concatenate([result_a, result_b], axis=0)


def halves(array, core):
    width = array.shape[1] // 2
    mine = lax.dynamic_slice_in_dim(array, core * width, width, axis=1)
    other = lax.dynamic_slice_in_dim(array, (1 - core) * width, width, axis=1)
    return mine, other


def local(queries, keys, values, out_weight):
    core = lax.rem(lax.axis_index("seq"), NC)
    k_mine, k_other = halves(keys, core)
    v_mine, v_other = halves(values, core)
    kv_mine = jnp.concatenate([k_mine, v_mine], axis=1)
    kv_other = jnp.concatenate([k_other, v_other], axis=1)
    near_unit = jnp.concatenate([kv_mine, swap(kv_other, 0, 1)], axis=0)
    far_unit = jnp.concatenate([swap(kv_mine, 1, 0), swap(kv_other, 1, 1)], axis=0)

    queries, _ = tie(queries, near_unit)
    q_mine, q_other = halves(queries, core)
    q_got = swap(q_other, 0, 1)
    q = jnp.concatenate([q_mine, q_got], axis=0)

    near = jnp.concatenate(line_of(near_unit), axis=0)
    near, far_unit = tie(near, far_unit)
    near_one, near_two = pair_second(near, 1), pair_second(near, -1)
    state = attend(q, None, [(units_at(0, 0), near)])
    far = jnp.concatenate(line_of(far_unit), axis=0)
    far, *state = tie(far, *state)
    far_one, far_two = pair_second(far, 1), pair_second(far, -1)
    state = attend(q, state, [(units_at(0, 1), far)])
    near_one, near_two, *state = tie(near_one, near_two, *state)
    half = UNIT * LINE // 2
    near_across = jnp.concatenate(
        [pair_second(near_one[:half], -1), pair_second(near_two[half:], 1)], axis=0
    )
    state = attend(q, state, [(units_at(1, 0), near_one), (units_at(-1, 0), near_two)])
    far_one, far_two, *state = tie(far_one, far_two, *state)
    far_across = jnp.concatenate(
        [pair_second(far_one[:half], -1), pair_second(far_two[half:], 1)], axis=0
    )
    state = attend(q, state, [(units_at(1, 1), far_one), (units_at(-1, 1), far_two)])
    state = attend(q, state, [(units_at(2, 0), near_across)])
    attended = attend(q, state, [(units_at(2, 1), far_across)], last=True)
    other = swap(attended[TOK:], 0, 1)
    return project_and_sum(attended[:TOK], other, out_weight)


def solution(mesh):
    placed = (P("seq", "head"), P("seq", "head"), P("seq", "head"), P("head", None))
    return jax.shard_map(
        local, mesh=mesh, in_specs=placed, out_specs=P("seq", "head"), check_vma=False
    )
```

```python
import functools
import math

import jax
import jax.numpy as jnp
from jax import lax
from jax.experimental import pallas as pl
from jax.experimental.pallas import tpu as pltpu
from jax.sharding import PartitionSpec as P

HEAD_DIM = 128
GROUP = 4
TOK = 192
UNIT = 2 * TOK
NX, NZ, NY, NC = 4, 2, 4, 2
NHEAD = 4
COLS = 1024
EXP_SCALE = math.log2(math.e) / math.sqrt(HEAD_DIM)
LOW = -1e30
BF16 = jnp.bfloat16
F32 = jnp.float32


def seq_of(x, z, y, c):
    return ((x % NX * NZ + z) * NY + y % NY) * NC + c


def seq_perm(move):
    pairs = []
    for x in range(NX):
        for z in range(NZ):
            for y in range(NY):
                for c in range(NC):
                    pairs.append((seq_of(x, z, y, c), seq_of(*move(x, z, y, c))))
    return pairs


def partner(place, d):
    return place + (d if place % 2 == 0 else -d)


def pair_first(data, d):
    move = lambda x, z, y, c: (x, z, partner(y, d), c) if c == 0 else (partner(x, d), z, y, c)
    return lax.ppermute(data, "seq", seq_perm(move))


def pair_second(data, d):
    move = lambda x, z, y, c: (partner(x, d), z, y, c) if c == 0 else (x, z, partner(y, d), c)
    return lax.ppermute(data, "seq", seq_perm(move))


def swap(data, dz, dc):
    move = lambda x, z, y, c: (x, z ^ dz, y, c ^ dc)
    return lax.ppermute(data, "seq", seq_perm(move))


def place():
    index = lax.axis_index("seq")
    core = lax.rem(index, NC)
    y = lax.rem(index // NC, NY)
    z = lax.rem(index // (NC * NY), NZ)
    x = index // (NC * NY * NZ)
    return x, z, y, core


def order_of(unit):
    first, second, dz = unit
    x, z, y, core = place()
    dx = jnp.where(core == 0, second, first) * (1 - 2 * lax.rem(x, 2))
    dy = jnp.where(core == 0, first, second) * (1 - 2 * lax.rem(y, 2))
    zz = 1 - z if dz else z
    return lax.rem(x + dx + NX, NX) * (NZ * NY) + zz * NY + lax.rem(y + dy + NY, NY)


HALF = TOK // 2
LINE = 4
STATE = (
    jax.ShapeDtypeStruct((GROUP * UNIT, HEAD_DIM), F32),
    jax.ShapeDtypeStruct((GROUP * UNIT, 2 * HEAD_DIM), F32),
)
VMEM = pl.BlockSpec(memory_space=pltpu.VMEM)
SHORT = pl.CostEstimate(flops=2**26, bytes_accessed=2**16, transcendentals=2**16)
LONG = pl.CostEstimate(flops=2**31, bytes_accessed=2**20, transcendentals=0)


def hidden_keys(kv_ref, allowed):
    columns = [jnp.full((UNIT, HEAD_DIM), jnp.where(a, 0.0, LOW), F32) for a in allowed]
    columns = jnp.concatenate(columns, axis=0).astype(BF16)
    return jnp.concatenate([kv_ref[:, :HEAD_DIM], columns], axis=1)


def own_bias():
    _, _, _, core = place()
    row = lax.broadcasted_iota(jnp.int32, (UNIT, UNIT), 0)
    col = lax.broadcasted_iota(jnp.int32, (UNIT, UNIT), 1)
    shift = jnp.where(core == 0, 0, TOK)
    row_pos = jnp.where(row < TOK, row + shift, row - shift)
    col_pos = jnp.where(col < TOK, col + shift, col - shift)
    return jnp.where(col_pos <= row_pos, 0.0, LOW).astype(F32)


def joined(pieces):
    return pieces[0] if len(pieces) == 1 else jnp.concatenate(pieces, axis=0)


def attend_kernel(lines, tiles, first, last, q_ref, *refs):
    refs = list(refs)
    kv_refs = [refs.pop(0) for _ in lines]
    state_in = None if first else (refs.pop(0), refs.pop(0))
    out_ref = refs.pop(0) if last else None
    state_out = refs
    mine = order_of((0, 0, 0))
    compute = functools.partial(
        attend_lines, lines, tiles, first, last, mine, q_ref, kv_refs, state_in, out_ref, state_out
    )
    if first:
        compute()
        return
    wanted = [order_of(unit) < mine for units in lines for unit in units]
    wanted = functools.reduce(jnp.logical_or, wanted)
    pl.when(wanted)(compute)

    @pl.when(jnp.logical_not(wanted))
    def _():
        if not last:
            state_out[0][...] = state_in[0][...]
            state_out[1][...] = state_in[1][...]
            return
        for tile in tiles:
            for head, rows in tile:
                total = state_in[1][pl.ds(head * UNIT + rows.start, rows.size), :]
                result = total[:, :HEAD_DIM] / total[:, HEAD_DIM:]
                out_ref[:, head * HEAD_DIM : (head + 1) * HEAD_DIM] = result.astype(BF16)


def attend_lines(
    lines, tiles, first, last, mine, q_ref, kv_refs, state_in, out_ref, state_out
):
    mark = lax.broadcasted_iota(jnp.int32, (UNIT, HEAD_DIM), 1) == 0
    mark = mark.astype(F32).astype(BF16)
    steps = [(line, tile) for line in range(len(lines)) for tile in tiles]
    keys, values = {}, {}

    def scores_of(step):
        line, tile = step
        if line not in keys:
            allowed = [order_of(unit) < mine for unit in lines[line]]
            if first and line == 0:
                allowed[0] = True
            keys[line] = hidden_keys(kv_refs[line], allowed)
            value = kv_refs[line][:, HEAD_DIM:]
            values[line] = jnp.concatenate([value, jnp.ones(value.shape, BF16)], axis=1)
        q = joined(
            [q_ref[rows, head * HEAD_DIM : (head + 1) * HEAD_DIM] for head, rows in tile]
        )
        scores = lax.dot_general(
            jnp.concatenate([q, mark], axis=1),
            keys[line],
            (((1,), (1,)), ((), ())),
            preferred_element_type=F32,
        )
        if first and line == 0:
            own = scores[:, :UNIT] + own_bias()
            scores = jnp.concatenate([own, scores[:, UNIT:]], axis=1)
        return scores

    ahead = scores_of(steps[0])
    for number, (line, tile) in enumerate(steps):
        scores = ahead
        if number + 1 < len(steps):
            ahead = scores_of(steps[number + 1])
        places = [pl.ds(head * UNIT + rows.start, rows.size) for head, rows in tile]
        state = state_in if line == 0 else state_out
        top = jnp.max(scores, axis=1, keepdims=True) * EXP_SCALE
        if state is not None:
            old = joined([state[0][rows, :1] for rows in places])
            top = jnp.maximum(old, top)
        weights = jnp.exp2(scores * EXP_SCALE - top).astype(BF16)
        product = jnp.dot(weights, values[line], preferred_element_type=F32)
        if state is not None:
            product += joined([state[1][rows, :] for rows in places]) * jnp.exp2(old - top)
        if last and line + 1 == len(lines):
            result = (product[:, :HEAD_DIM] / product[:, HEAD_DIM:]).astype(BF16)
            for i, (head, rows) in enumerate(tile):
                out_ref[:, head * HEAD_DIM : (head + 1) * HEAD_DIM] = result[
                    i * rows.size : (i + 1) * rows.size
                ]
        else:
            top = jnp.broadcast_to(top, (UNIT, HEAD_DIM))
            for i, rows in enumerate(places):
                state_out[0][rows, :] = top[i * rows.size : (i + 1) * rows.size]
                state_out[1][rows, :] = product[i * rows.size : (i + 1) * rows.size]


WHOLE = [[(head, pl.ds(0, UNIT))] for head in range(GROUP)]


def tiles_of(start):
    rows = pl.ds(start, TOK)
    return [[(head, rows), (head + 1, rows)] for head in range(0, GROUP, 2)]


def attend(q, state, lines, tiles=None, cost=SHORT):
    last = tiles is not None
    if last:
        out_shape = jax.ShapeDtypeStruct((TOK, GROUP * HEAD_DIM), BF16)
        out_specs = VMEM
        scratch = [pltpu.VMEM(s.shape, s.dtype) for s in STATE]
    else:
        out_shape = STATE
        out_specs = (VMEM, VMEM)
        scratch = []
    args = [q, *(data for _, data in lines), *(state or ())]
    units = [u for u, _ in lines]
    return pl.pallas_call(
        functools.partial(attend_kernel, units, tiles or WHOLE, state is None, last),
        out_shape=out_shape,
        in_specs=[VMEM] * len(args),
        out_specs=out_specs,
        scratch_shapes=scratch,
        compiler_params=pltpu.CompilerParams(vmem_limit_bytes=24 * 2**20),
        cost_estimate=cost,
        name="attend",
    )(*args)


OFFSETS = (0, 1, -1, 2)


def units_at(second, dz):
    return tuple((first, second, dz) for first in OFFSETS)


def line_of(unit):
    return (unit, pair_first(unit, 1), pair_first(unit, -1), pair_first(unit, 2))


def tie(*arrays):
    return lax.optimization_barrier(arrays)


def after(array, earlier):
    return tie(array, earlier)[0]


def chunk_of(turn):
    head = lax.axis_index("head")
    chunk = jnp.int32(TURNS[0][turn])
    for number in range(1, NHEAD):
        chunk = jnp.where(head == number, TURNS[number][turn], chunk)
    return chunk


def project_kernel(turns, mine_ref, other_ref, w_ref, *out_refs):
    _, _, _, core = place()
    half = GROUP * HEAD_DIM
    first = pl.multiple_of(core * half, half)
    second = pl.multiple_of((1 - core) * half, half)
    for number, turn in enumerate(turns):
        columns = pl.ds(pl.multiple_of(chunk_of(turn) * COLS, COLS), COLS)
        total = jnp.dot(
            mine_ref[...], w_ref[pl.ds(first, half), columns], preferred_element_type=F32
        )
        total += jnp.dot(
            other_ref[...], w_ref[pl.ds(second, half), columns], preferred_element_type=F32
        )
        total = total.astype(BF16)
        out_refs[2 * number][...] = total[:HALF]
        out_refs[2 * number + 1][...] = total[HALF:]


def project(turns, mine, other, weight):
    count = 2 * len(turns)
    return pl.pallas_call(
        functools.partial(project_kernel, turns),
        out_shape=[jax.ShapeDtypeStruct((HALF, COLS), BF16)] * count,
        in_specs=[VMEM] * 3,
        out_specs=[VMEM] * count,
        compiler_params=pltpu.CompilerParams(vmem_limit_bytes=24 * 2**20),
        cost_estimate=LONG,
        name="project",
    )(mine, other, weight)


def add(*terms):
    total = terms[0].astype(F32)
    for term in terms[1:]:
        total = total + term.astype(F32)
    return total.astype(BF16)


TURNS = ((3, 2, 1, 0), (3, 2, 0, 1), (0, 1, 3, 2), (0, 1, 2, 3))


def outer(data):
    return lax.ppermute(data, "head", [(3, 2), (2, 3), (1, 0), (0, 1)])


def inner(data):
    return lax.ppermute(data, "head", [(2, 1), (1, 2)])


def project_and_sum(mine, other, weight):
    a_0, b_0 = project((0,), mine, other, weight)
    outer_0a, outer_0b = outer(a_0), outer(b_0)
    mine, a_0 = tie(mine, a_0)
    a_1, b_1, a_2, b_2, a_3, b_3 = project((1, 2, 3), mine, other, weight)
    outer_1a, outer_1b = outer(a_1), outer(b_1)
    sum_0a, sum_0b = add(a_0, outer_0a), add(b_0, outer_0b)
    sum_0a, a_1, b_1 = tie(sum_0a, a_1, b_1)
    inner_0a = inner(sum_0a)
    inner_0b = inner(after(sum_0b, sum_0a))
    sum_1a = after(add(a_1, outer_1a), sum_0b)
    inner_1a = inner(sum_1a)
    sum_2a = add(a_2, inner_0a)
    outer_2a = outer(sum_2a)
    sum_1b = after(add(b_1, outer_1b), sum_2a)
    inner_1b = inner(sum_1b)
    outer_2b = outer(add(b_2, inner_0b))
    result_a = add(a_3, outer_2a, inner_1a)
    result_b = add(b_3, outer_2b, inner_1b)
    return jnp.concatenate([result_a, result_b], axis=0)


def halves(array, core):
    width = array.shape[1] // 2
    mine = lax.dynamic_slice_in_dim(array, core * width, width, axis=1)
    other = lax.dynamic_slice_in_dim(array, (1 - core) * width, width, axis=1)
    return mine, other


def local(queries, keys, values, out_weight):
    core = lax.rem(lax.axis_index("seq"), NC)
    k_mine, k_other = halves(keys, core)
    v_mine, v_other = halves(values, core)
    kv_mine = jnp.concatenate([k_mine, v_mine], axis=1)
    kv_other = jnp.concatenate([k_other, v_other], axis=1)
    near_unit = jnp.concatenate([kv_mine, swap(kv_other, 0, 1)], axis=0)
    far_unit = jnp.concatenate([swap(kv_mine, 1, 0), swap(kv_other, 1, 1)], axis=0)

    queries, _ = tie(queries, near_unit)
    q_mine, q_other = halves(queries, core)
    q_got = swap(q_other, 0, 1)
    q = jnp.concatenate([q_mine, q_got], axis=0)

    near = jnp.concatenate(line_of(near_unit), axis=0)
    near, far_unit = tie(near, far_unit)
    near_one, near_two = pair_second(near, 1), pair_second(near, -1)
    state = attend(q, None, [(units_at(0, 0), near)])
    far = jnp.concatenate(line_of(far_unit), axis=0)
    far, *state = tie(far, *state)
    far_one, far_two = pair_second(far, 1), pair_second(far, -1)
    state = attend(q, state, [(units_at(0, 1), far)])
    near_one, near_two, *state = tie(near_one, near_two, *state)
    half = UNIT * LINE // 2
    near_across = jnp.concatenate(
        [pair_second(near_one[:half], -1), pair_second(near_two[half:], 1)], axis=0
    )
    state = attend(q, state, [(units_at(1, 0), near_one), (units_at(-1, 0), near_two)])
    far_one, far_two, *state = tie(far_one, far_two, *state)
    far_across = jnp.concatenate(
        [pair_second(far_one[:half], -1), pair_second(far_two[half:], 1)], axis=0
    )
    state = attend(q, state, [(units_at(1, 1), far_one), (units_at(-1, 1), far_two)])
    state = attend(q, state, [(units_at(2, 0), near_across)])
    theirs = attend(q, state, [(units_at(2, 1), far_across)], tiles_of(TOK))
    other = swap(theirs, 0, 1)
    q = after(q, theirs)
    mine = attend(q, state, [(units_at(2, 1), far_across)], tiles_of(0), LONG)
    return project_and_sum(mine, other, out_weight)


def solution(mesh):
    placed = (P("seq", "head"), P("seq", "head"), P("seq", "head"), P("head", None))
    return jax.shard_map(
        local, mesh=mesh, in_specs=placed, out_specs=P("seq", "head"), check_vma=False
    )
```

```python
import functools
import math

import jax
import jax.numpy as jnp
from jax import lax
from jax.experimental import pallas as pl
from jax.experimental.pallas import tpu as pltpu
from jax.sharding import PartitionSpec as P

HEAD_DIM = 128
GROUP = 4
TOK = 192
UNIT = 2 * TOK
NX, NZ, NY, NC = 4, 2, 4, 2
NHEAD = 4
COLS = 1024
EXP_SCALE = math.log2(math.e) / math.sqrt(HEAD_DIM)
LOW = -1e30
BF16 = jnp.bfloat16
F32 = jnp.float32


def seq_of(x, z, y, c):
    return ((x % NX * NZ + z) * NY + y % NY) * NC + c


def seq_perm(move):
    pairs = []
    for x in range(NX):
        for z in range(NZ):
            for y in range(NY):
                for c in range(NC):
                    pairs.append((seq_of(x, z, y, c), seq_of(*move(x, z, y, c))))
    return pairs


def partner(place, d):
    return place + (d if place % 2 == 0 else -d)


def pair_first(data, d):
    move = lambda x, z, y, c: (x, z, partner(y, d), c) if c == 0 else (partner(x, d), z, y, c)
    return lax.ppermute(data, "seq", seq_perm(move))


def pair_second(data, d):
    move = lambda x, z, y, c: (partner(x, d), z, y, c) if c == 0 else (x, z, partner(y, d), c)
    return lax.ppermute(data, "seq", seq_perm(move))


def swap(data, dz, dc):
    move = lambda x, z, y, c: (x, z ^ dz, y, c ^ dc)
    return lax.ppermute(data, "seq", seq_perm(move))


def place():
    index = lax.axis_index("seq")
    core = lax.rem(index, NC)
    y = lax.rem(index // NC, NY)
    z = lax.rem(index // (NC * NY), NZ)
    x = index // (NC * NY * NZ)
    return x, z, y, core


def order_of(unit):
    first, second, dz = unit
    x, z, y, core = place()
    dx = jnp.where(core == 0, second, first) * (1 - 2 * lax.rem(x, 2))
    dy = jnp.where(core == 0, first, second) * (1 - 2 * lax.rem(y, 2))
    zz = 1 - z if dz else z
    return lax.rem(x + dx + NX, NX) * (NZ * NY) + zz * NY + lax.rem(y + dy + NY, NY)


HALF = TOK // 2
LINE = 4
STATE = (
    jax.ShapeDtypeStruct((GROUP * UNIT, HEAD_DIM), F32),
    jax.ShapeDtypeStruct((GROUP * UNIT, 2 * HEAD_DIM), F32),
)
VMEM = pl.BlockSpec(memory_space=pltpu.VMEM)
SHORT = pl.CostEstimate(flops=2**26, bytes_accessed=2**16, transcendentals=2**16)
LONG = pl.CostEstimate(flops=2**31, bytes_accessed=2**20, transcendentals=0)


def hidden_keys(kv_ref, allowed):
    columns = [jnp.full((UNIT, HEAD_DIM), jnp.where(a, 0.0, LOW), F32) for a in allowed]
    columns = jnp.concatenate(columns, axis=0).astype(BF16)
    return jnp.concatenate([kv_ref[:, :HEAD_DIM], columns], axis=1)


def own_bias():
    _, _, _, core = place()
    row = lax.broadcasted_iota(jnp.int32, (UNIT, UNIT), 0)
    col = lax.broadcasted_iota(jnp.int32, (UNIT, UNIT), 1)
    shift = jnp.where(core == 0, 0, TOK)
    row_pos = jnp.where(row < TOK, row + shift, row - shift)
    col_pos = jnp.where(col < TOK, col + shift, col - shift)
    return jnp.where(col_pos <= row_pos, 0.0, LOW).astype(F32)


def joined(pieces):
    return pieces[0] if len(pieces) == 1 else jnp.concatenate(pieces, axis=0)


def attend_kernel(lines, tiles, first, last, q_ref, *refs):
    refs = list(refs)
    kv_refs = [refs.pop(0) for _ in lines]
    state_in = None if first else (refs.pop(0), refs.pop(0))
    out_ref = refs.pop(0) if last else None
    state_out = refs
    mine = order_of((0, 0, 0))
    seen = [
        functools.reduce(jnp.logical_or, [order_of(unit) < mine for unit in units])
        for units in lines
    ]

    def compute(some):
        attend_lines(
            [lines[i] for i in some],
            tiles,
            first,
            last,
            mine,
            q_ref,
            [kv_refs[i] for i in some],
            state_in,
            out_ref,
            state_out,
        )

    if first:
        compute([0])
        return
    wanted = functools.reduce(jnp.logical_or, seen)
    if len(lines) == 1:
        pl.when(wanted)(lambda: compute([0]))
    else:
        pl.when(seen[0] & seen[1])(lambda: compute([0, 1]))
        pl.when(seen[0] & jnp.logical_not(seen[1]))(lambda: compute([0]))
        pl.when(seen[1] & jnp.logical_not(seen[0]))(lambda: compute([1]))

    @pl.when(jnp.logical_not(wanted))
    def _():
        if not last:
            state_out[0][...] = state_in[0][...]
            state_out[1][...] = state_in[1][...]
            return
        for tile in tiles:
            for head, rows in tile:
                total = state_in[1][pl.ds(head * UNIT + rows.start, rows.size), :]
                result = total[:, :HEAD_DIM] / total[:, HEAD_DIM:]
                out_ref[:, head * HEAD_DIM : (head + 1) * HEAD_DIM] = result.astype(BF16)


def attend_lines(
    lines, tiles, first, last, mine, q_ref, kv_refs, state_in, out_ref, state_out
):
    mark = lax.broadcasted_iota(jnp.int32, (UNIT, HEAD_DIM), 1) == 0
    mark = mark.astype(F32).astype(BF16)
    steps = [(line, tile) for line in range(len(lines)) for tile in tiles]
    keys, values = {}, {}

    def scores_of(step):
        line, tile = step
        if line not in keys:
            allowed = [order_of(unit) < mine for unit in lines[line]]
            if first and line == 0:
                allowed[0] = True
            keys[line] = hidden_keys(kv_refs[line], allowed)
            value = kv_refs[line][:, HEAD_DIM:]
            values[line] = jnp.concatenate([value, jnp.ones(value.shape, BF16)], axis=1)
        q = joined(
            [q_ref[rows, head * HEAD_DIM : (head + 1) * HEAD_DIM] for head, rows in tile]
        )
        scores = lax.dot_general(
            jnp.concatenate([q, mark], axis=1),
            keys[line],
            (((1,), (1,)), ((), ())),
            preferred_element_type=F32,
        )
        if first and line == 0:
            own = scores[:, :UNIT] + own_bias()
            scores = jnp.concatenate([own, scores[:, UNIT:]], axis=1)
        return scores

    ahead = scores_of(steps[0])
    for number, (line, tile) in enumerate(steps):
        scores = ahead
        if number + 1 < len(steps):
            ahead = scores_of(steps[number + 1])
        places = [pl.ds(head * UNIT + rows.start, rows.size) for head, rows in tile]
        state = state_in if line == 0 else state_out
        top = jnp.max(scores, axis=1, keepdims=True) * EXP_SCALE
        if state is not None:
            old = joined([state[0][rows, :1] for rows in places])
            top = jnp.maximum(old, top)
        weights = jnp.exp2(scores * EXP_SCALE - top).astype(BF16)
        product = jnp.dot(weights, values[line], preferred_element_type=F32)
        if state is not None:
            product += joined([state[1][rows, :] for rows in places]) * jnp.exp2(old - top)
        if last and line + 1 == len(lines):
            result = (product[:, :HEAD_DIM] / product[:, HEAD_DIM:]).astype(BF16)
            for i, (head, rows) in enumerate(tile):
                out_ref[:, head * HEAD_DIM : (head + 1) * HEAD_DIM] = result[
                    i * rows.size : (i + 1) * rows.size
                ]
        else:
            top = jnp.broadcast_to(top, (UNIT, HEAD_DIM))
            for i, rows in enumerate(places):
                state_out[0][rows, :] = top[i * rows.size : (i + 1) * rows.size]
                state_out[1][rows, :] = product[i * rows.size : (i + 1) * rows.size]


WHOLE = [[(head, pl.ds(0, UNIT))] for head in range(GROUP)]


def tiles_of(start):
    rows = pl.ds(start, TOK)
    return [[(head, rows), (head + 1, rows)] for head in range(0, GROUP, 2)]


def attend(q, state, lines, tiles=None, cost=SHORT):
    last = tiles is not None
    if last:
        out_shape = jax.ShapeDtypeStruct((TOK, GROUP * HEAD_DIM), BF16)
        out_specs = VMEM
        scratch = [pltpu.VMEM(s.shape, s.dtype) for s in STATE]
    else:
        out_shape = STATE
        out_specs = (VMEM, VMEM)
        scratch = []
    args = [q, *(data for _, data in lines), *(state or ())]
    units = [u for u, _ in lines]
    return pl.pallas_call(
        functools.partial(attend_kernel, units, tiles or WHOLE, state is None, last),
        out_shape=out_shape,
        in_specs=[VMEM] * len(args),
        out_specs=out_specs,
        scratch_shapes=scratch,
        compiler_params=pltpu.CompilerParams(vmem_limit_bytes=24 * 2**20),
        cost_estimate=cost,
        name="attend",
    )(*args)


OFFSETS = (0, 1, -1, 2)


def units_at(second, dz):
    return tuple((first, second, dz) for first in OFFSETS)


def line_of(unit):
    return (unit, pair_first(unit, 1), pair_first(unit, -1), pair_first(unit, 2))


def tie(*arrays):
    return lax.optimization_barrier(arrays)


def after(array, earlier):
    return tie(array, earlier)[0]


def chunk_of(turn):
    head = lax.axis_index("head")
    chunk = jnp.int32(TURNS[0][turn])
    for number in range(1, NHEAD):
        chunk = jnp.where(head == number, TURNS[number][turn], chunk)
    return chunk


def project_kernel(turns, mine_ref, other_ref, w_ref, *out_refs):
    _, _, _, core = place()
    half = GROUP * HEAD_DIM
    first = pl.multiple_of(core * half, half)
    second = pl.multiple_of((1 - core) * half, half)
    for number, turn in enumerate(turns):
        columns = pl.ds(pl.multiple_of(chunk_of(turn) * COLS, COLS), COLS)
        total = jnp.dot(
            mine_ref[...], w_ref[pl.ds(first, half), columns], preferred_element_type=F32
        )
        total += jnp.dot(
            other_ref[...], w_ref[pl.ds(second, half), columns], preferred_element_type=F32
        )
        total = total.astype(BF16)
        out_refs[2 * number][...] = total[:HALF]
        out_refs[2 * number + 1][...] = total[HALF:]


def project(turns, mine, other, weight):
    count = 2 * len(turns)
    return pl.pallas_call(
        functools.partial(project_kernel, turns),
        out_shape=[jax.ShapeDtypeStruct((HALF, COLS), BF16)] * count,
        in_specs=[VMEM] * 3,
        out_specs=[VMEM] * count,
        compiler_params=pltpu.CompilerParams(vmem_limit_bytes=24 * 2**20),
        cost_estimate=LONG,
        name="project",
    )(mine, other, weight)


def add(*terms):
    total = terms[0].astype(F32)
    for term in terms[1:]:
        total = total + term.astype(F32)
    return total.astype(BF16)


TURNS = ((3, 2, 1, 0), (3, 2, 0, 1), (0, 1, 3, 2), (0, 1, 2, 3))


def outer(data):
    return lax.ppermute(data, "head", [(3, 2), (2, 3), (1, 0), (0, 1)])


def inner(data):
    return lax.ppermute(data, "head", [(2, 1), (1, 2)])


def project_and_sum(mine, other, weight):
    a_0, b_0 = project((0,), mine, other, weight)
    outer_0a, outer_0b = outer(a_0), outer(b_0)
    mine, a_0 = tie(mine, a_0)
    a_1, b_1, a_2, b_2, a_3, b_3 = project((1, 2, 3), mine, other, weight)
    outer_1a, outer_1b = outer(a_1), outer(b_1)
    sum_0a, sum_0b = add(a_0, outer_0a), add(b_0, outer_0b)
    sum_0a, a_1, b_1 = tie(sum_0a, a_1, b_1)
    inner_0a = inner(sum_0a)
    inner_0b = inner(after(sum_0b, sum_0a))
    sum_1a = after(add(a_1, outer_1a), sum_0b)
    inner_1a = inner(sum_1a)
    sum_2a = add(a_2, inner_0a)
    outer_2a = outer(sum_2a)
    sum_1b = after(add(b_1, outer_1b), sum_2a)
    inner_1b = inner(sum_1b)
    outer_2b = outer(add(b_2, inner_0b))
    result_a = add(a_3, outer_2a, inner_1a)
    result_b = add(b_3, outer_2b, inner_1b)
    return jnp.concatenate([result_a, result_b], axis=0)


def halves(array, core):
    width = array.shape[1] // 2
    mine = lax.dynamic_slice_in_dim(array, core * width, width, axis=1)
    other = lax.dynamic_slice_in_dim(array, (1 - core) * width, width, axis=1)
    return mine, other


def local(queries, keys, values, out_weight):
    core = lax.rem(lax.axis_index("seq"), NC)
    k_mine, k_other = halves(keys, core)
    v_mine, v_other = halves(values, core)
    kv_mine = jnp.concatenate([k_mine, v_mine], axis=1)
    kv_other = jnp.concatenate([k_other, v_other], axis=1)
    near_unit = jnp.concatenate([kv_mine, swap(kv_other, 0, 1)], axis=0)
    far_unit = jnp.concatenate([swap(kv_mine, 1, 0), swap(kv_other, 1, 1)], axis=0)

    queries, _ = tie(queries, near_unit)
    q_mine, q_other = halves(queries, core)
    q_got = swap(q_other, 0, 1)
    q = jnp.concatenate([q_mine, q_got], axis=0)

    near = jnp.concatenate(line_of(near_unit), axis=0)
    near, far_unit = tie(near, far_unit)
    near_one, near_two = pair_second(near, 1), pair_second(near, -1)
    state = attend(q, None, [(units_at(0, 0), near)])
    far = jnp.concatenate(line_of(far_unit), axis=0)
    far, *state = tie(far, *state)
    far_one, far_two = pair_second(far, 1), pair_second(far, -1)
    state = attend(q, state, [(units_at(0, 1), far)])
    near_one, near_two, *state = tie(near_one, near_two, *state)
    half = UNIT * LINE // 2
    near_across = jnp.concatenate(
        [pair_second(near_one[:half], -1), pair_second(near_two[half:], 1)], axis=0
    )
    state = attend(q, state, [(units_at(1, 0), near_one), (units_at(-1, 0), near_two)])
    far_one, far_two, *state = tie(far_one, far_two, *state)
    far_across = jnp.concatenate(
        [pair_second(far_one[:half], -1), pair_second(far_two[half:], 1)], axis=0
    )
    state = attend(q, state, [(units_at(1, 1), far_one), (units_at(-1, 1), far_two)])
    state = attend(q, state, [(units_at(2, 0), near_across)])
    theirs = attend(q, state, [(units_at(2, 1), far_across)], tiles_of(TOK))
    other = swap(theirs, 0, 1)
    q = after(q, theirs)
    mine = attend(q, state, [(units_at(2, 1), far_across)], tiles_of(0), LONG)
    return project_and_sum(mine, other, out_weight)


def solution(mesh):
    placed = (P("seq", "head"), P("seq", "head"), P("seq", "head"), P("head", None))
    return jax.shard_map(
        local, mesh=mesh, in_specs=placed, out_specs=P("seq", "head"), check_vma=False
    )
```
